256 devices in a mesh: inner: 16 (over z, core), outer: 2 (over y_hi), head: 8 (over x, y_lo).
Axes of the slice: x: 4, y: 4 (y_hi: 2, y_lo: 2; y = y_hi * 2 + y_lo), z: 8, core: 2. Of those that a mesh axis runs over, the one named last changes fastest.
Arguments:
- queries: bfloat16 [8192, 24, 128], P(('inner', 'outer'), 'head'), may hold values from -5.1 to 5.1
- keys: bfloat16 [8192, 24, 128], P(('inner', 'outer'), 'head'), may hold values from -5.1 to 5.1
- values: bfloat16 [8192, 24, 128], P(('inner', 'outer'), 'head'), may hold values from -6 to 6
- forward_out: bfloat16 [8192, 24, 128], P(('inner', 'outer'), 'head'), may hold values from -6 to 6
- out_grad: bfloat16 [8192, 24, 128], P(('inner', 'outer'), 'head'), may hold values from -6 to 6
- span_order: int32 [32], replicated, may hold values from 0 to 31, each once
- block_mask: int32 [64, 64], replicated, may hold values from 0 to 1, as said below
Outputs:
- grad_queries: bfloat16 [8192, 24, 128], P(('inner', 'outer'), 'head')
- grad_keys: bfloat16 [8192, 24, 128], P(('inner', 'outer'), 'head')
- grad_values: bfloat16 [8192, 24, 128], P(('inner', 'outer'), 'head')
The draws below stay inside these ranges and needn't reach their ends.
Inputs may be any that keep to these rules, and one draw needn't show every extreme that they name: `span_order`: each of 0 to 31 once. `block_mask`: 0 or 1; every block may attend to itself.
All inputs are finite; a program needn't handle non-finite values.
Results may differ from the reference program's by a relative error of at most 0.005.
Values may be sent and summed in bfloat16 or wider, within the bound.
No kernel may reach another device: no remote copies, remote signals or barrier semaphores. Data moves between devices by JAX's collectives and lax.ppermute only.
A program may use at most 128 MiB of HBM per device.

```python
import jax
import jax.numpy as jnp
from jax import lax

HEADS = 24
HD = 128
S_DEV = 256
BLOCK = 128
SPANS = 32
TOKENS = 8192
NBLK = 64


def draw_queries(key, part):
    key = jax.random.fold_in(key, 1)
    base = jnp.clip(jax.random.normal(key, (TOKENS, HEADS, HD), jnp.float32), -5.0, 5.0)
    return base.astype(jnp.bfloat16)


def draw_keys(key, part):
    key = jax.random.fold_in(key, 2)
    base = jnp.clip(jax.random.normal(key, (TOKENS, HEADS, HD), jnp.float32), -5.0, 5.0)
    return base.astype(jnp.bfloat16)


def draw_block_mask(key, part):
    key = jax.random.fold_in(key, 3)
    index = jnp.arange(NBLK, dtype=jnp.int32)
    band = jnp.abs(index[:, None] - index[None, :]) <= 2
    extra = jax.random.randint(key, (NBLK, NBLK), 0, 4) == 0
    return jnp.where(band | extra, 1, 0).astype(jnp.int32)


def block_scale(own_key, shape, pieces, least, top_value):
    gain = 1.0
    for axis_at, blocks in pieces:
        draws = jax.random.uniform(jax.random.fold_in(jax.random.fold_in(own_key, 6), axis_at), (blocks,), jnp.float32, least / len(pieces), top_value / len(pieces))
        gain = gain * jnp.repeat(jnp.exp(draws), shape[axis_at] // blocks).reshape((-1,) + (1,) * (len(shape) - 1 - axis_at))
    return gain


def gaussian(key, shape, deviation, limit, split=(), kind=jnp.bfloat16):
    values = deviation * jax.random.normal(key, shape, jnp.float32)
    if split:
        values = values * block_scale(key, shape, split, -0.22, 0.18)
    return jnp.clip(values, -limit, limit).astype(kind)


def setup_inputs(seed: int = 0) -> dict:
    splits = jax.random.split(jax.random.key(seed), 8)
    queries = draw_queries(jax.random.fold_in(splits[7], 71), 0)
    keys = draw_keys(jax.random.fold_in(splits[7], 71), 0)
    values = gaussian(splits[2], (TOKENS, HEADS, HD), 1.0, 6.0, ((0, 32), (1, 8)))
    forward_out = gaussian(splits[3], (TOKENS, HEADS, HD), 1.0, 6.0, ((0, 32), (1, 8)))
    out_grad = gaussian(splits[4], (TOKENS, HEADS, HD), 1.0, 6.0, ((0, 32), (1, 8)))
    span_order = jax.random.permutation(splits[5], SPANS).astype(jnp.int32)
    block_mask = draw_block_mask(jax.random.fold_in(splits[7], 71), 0)
    return dict(queries=queries, keys=keys, values=values, forward_out=forward_out, out_grad=out_grad, span_order=span_order, block_mask=block_mask)


neg_fill = -1e30


def reference(queries, keys, values, forward_out, out_grad, span_order, block_mask):
    scale = HD ** -0.5
    positions = jnp.arange(TOKENS, dtype=jnp.int32)
    global_block = span_order[positions // S_DEV].astype(jnp.int32) * (S_DEV // BLOCK) + (positions % S_DEV) // BLOCK
    linked = block_mask[global_block][:, global_block] > 0

    def one_head(items):
        query_head, key_head, value_head, fwd_head, grad_head = items
        scores = jnp.dot(query_head, key_head.T, preferred_element_type=jnp.float32) * scale
        scores = jnp.where(linked, scores, neg_fill)
        peak = jnp.max(scores, axis=1)
        lse = peak + jnp.log(jnp.sum(jnp.exp(scores - peak[:, None]), axis=1))
        probs = jnp.where(linked, jnp.exp(scores - lse[:, None]), 0.0)
        rounded = probs.astype(jnp.bfloat16)
        delta = jnp.sum(grad_head.astype(jnp.float32) * fwd_head.astype(jnp.float32), axis=1)
        dprobs = jnp.dot(grad_head, value_head.T, preferred_element_type=jnp.float32)
        dscores = (probs * (dprobs - delta[:, None])).astype(jnp.bfloat16)
        grad_query = (jnp.dot(dscores, key_head, preferred_element_type=jnp.float32) * scale).astype(jnp.bfloat16)
        grad_key = (jnp.dot(dscores.T, query_head, preferred_element_type=jnp.float32) * scale).astype(jnp.bfloat16)
        grad_value = jnp.dot(rounded.T, grad_head, preferred_element_type=jnp.float32).astype(jnp.bfloat16)
        return grad_query, grad_key, grad_value

    stacked = (queries.transpose(1, 0, 2), keys.transpose(1, 0, 2), values.transpose(1, 0, 2), forward_out.transpose(1, 0, 2), out_grad.transpose(1, 0, 2))
    grad_query, grad_key, grad_value = lax.map(one_head, stacked)
    return grad_query.transpose(1, 0, 2), grad_key.transpose(1, 0, 2), grad_value.transpose(1, 0, 2)
```

```python
import functools
import math

import jax
import jax.numpy as jnp
from jax import lax
from jax.experimental import pallas as pl
from jax.experimental.pallas import tpu as pltpu
from jax.sharding import PartitionSpec as P

BLOCK = 128
EMPTY = -1e30
VMEM_BYTES = 48 * 1024 * 1024
ZS = 8


def dot_t(a, b):
    return lax.dot_general(a, b, (((1,), (1,)), ((), ())), preferred_element_type=jnp.float32)


def list_links(where, span, mask, chunks, near, keys, zs):
    z, core, outer = where[0], where[1], where[2]
    columns = []
    for s in keys:
        piece = z * 4 + (core ^ (s // 2)) * 2 + (outer ^ (s % 2))
        for half in range(2):
            columns.append(span[piece] * 2 + half)
    chunks[0] = chunks[1] = 0
    count = jnp.int32(2)
    for slot, r in enumerate(near):
        row = span[lax.rem(z + r, zs) * 4 + core * 2 + outer] * 2
        for kb in range(len(columns)):
            halves = mask[row, columns[kb]] + 2 * mask[row + 1, columns[kb]]
            chunks[count] = halves * 64 + slot * 8 + kb
            count = count + jnp.minimum(halves, 1)
    chunks[count] = 0
    chunks[count + 1] = 0
    return count


def unlinked(chunk, rows):
    first = lax.broadcasted_iota(jnp.int32, (1, rows), 1) < BLOCK
    halves = chunk // 64
    return (chunk // 8) % 8, chunk % 8, jnp.where(first, halves % 2, halves // 2) == 0


def start(copies, sems):
    started = [pltpu.make_async_copy(src, dst, sems.at[i]) for i, (src, dst) in enumerate(copies)]
    for copy in started:
        copy.start()
    return started


def zero(*refs):
    for ref in refs:
        ref[...] = jnp.zeros_like(ref)


def set_delta(x, delta, rows):
    for i in range(x.shape[0]):
        for h in range(x.shape[1]):
            parts = x[i, h, 2 * rows :, :].astype(jnp.float32)
            parts = parts[0:2] + parts[2:4] + parts[4:6]
            delta[i, h] = jnp.concatenate([parts[0:1], parts[1:2]], axis=1)


def queries_kernel(near, where, span, mask, *refs):
    n = len(near)
    x_in, kv_in = refs[:n], refs[n : n + 4]
    dq, lse = refs[n + 4], refs[n + 5]
    x, kv, kt, delta, top, total, decay, products, dprobs, dscores, chunks, sems = refs[n + 6 :]
    heads, rows, width = kv.shape[1] // 2, kv.shape[2], kv.shape[3]
    copies = start(
        [(a, x.at[i]) for i, a in enumerate(x_in)] + [(a, kv.at[i]) for i, a in enumerate(kv_in)],
        sems,
    )
    scale = 1.0 / math.sqrt(width)
    factor = math.log2(math.e) * scale
    zero(dq, total, products, dprobs, dscores)
    top[...] = jnp.full_like(top, EMPTY)
    decay[...] = jnp.ones_like(decay)
    count = list_links(where, span, mask, chunks, near, range(4), ZS)
    for copy in copies:
        copy.wait()
    for s in range(4):
        for h in range(heads):
            for half in range(2):
                kt[s * 2 + half, h] = kv[s, h, half * BLOCK : (half + 1) * BLOCK, :].T
    set_delta(x, delta, rows)

    def body(i, _):
        at, kb, _ = unlinked(chunks[i], rows)
        for h in range(heads):
            dq[at, h] = dq[at, h] * decay[h] + jnp.dot(
                kt[kb, h], dscores[h], preferred_element_type=jnp.float32
            )
        at, kb, off = unlinked(chunks[i + 1], rows)
        for h in range(heads):
            scores = products[h] * factor
            old = top[at, h]
            new = jnp.where(off, old, jnp.maximum(old, jnp.max(scores, axis=0, keepdims=True)))
            probs = jnp.exp2(scores - jnp.where(off, -EMPTY, new))
            decay[h] = jnp.exp2(old - new)
            total[at, h] = total[at, h] * decay[h] + jnp.sum(probs, axis=0, keepdims=True)
            top[at, h] = new
            dscores[h] = (probs * (dprobs[h] - delta[at, h])).astype(jnp.bfloat16)
        at, kb, _ = unlinked(chunks[i + 2], rows)
        for h in range(heads):
            krows = pl.ds((kb % 2) * BLOCK, BLOCK)
            products[h] = dot_t(kv[kb // 2, h, krows, :], x[at, h, :rows])
            dprobs[h] = dot_t(kv[kb // 2, heads + h, krows, :], x[at, h, rows : 2 * rows])
        return 0

    lax.fori_loop(0, count, body, 0)
    for i in range(n):
        for h in range(heads):
            some = total[i, h] > 0
            safe = jnp.where(some, total[i, h], 1.0)
            lse[i, h : h + 1] = jnp.where(some, top[i, h] + jnp.log2(safe), EMPTY)
            dq[i, h] = dq[i, h] * (scale / safe)


def keys_kernel(keys, where, span, mask, lse, *refs):
    n, m = ZS, len(keys)
    x_in, kv_in = refs[:n], refs[n : n + m]
    dkv = refs[n + m]
    x, kv, delta, logs, products, dprobs, rounded, dscores, chunks, sems = refs[n + m + 1 :]
    heads, rows, width = kv.shape[1] // 2, kv.shape[2], kv.shape[3]
    copies = start(
        [(a, x.at[i]) for i, a in enumerate(x_in)] + [(a, kv.at[i]) for i, a in enumerate(kv_in)],
        sems,
    )
    factor = math.log2(math.e) / math.sqrt(width)
    zero(dkv, products, dprobs, rounded, dscores)
    count = list_links(where, span, mask, chunks, range(n), keys, ZS)
    for i in range(n):
        for h in range(heads):
            logs[i, h] = lse[i, h : h + 1]
    for copy in copies:
        copy.wait()
    set_delta(x, delta, rows)

    def body(i, _):
        at, kb, _ = unlinked(chunks[i], rows)
        krows = pl.ds((kb % 2) * BLOCK, BLOCK)
        for h in range(heads):
            dkv[kb // 2, heads + h, krows, :] += jnp.dot(
                rounded[h], x[at, h, rows : 2 * rows], preferred_element_type=jnp.float32
            )
            dkv[kb // 2, h, krows, :] += jnp.dot(
                dscores[h], x[at, h, :rows], preferred_element_type=jnp.float32
            )
        at, kb, off = unlinked(chunks[i + 1], rows)
        for h in range(heads):
            probs = jnp.exp2(products[h] * factor - jnp.where(off, -EMPTY, logs[at, h]))
            rounded[h] = probs.astype(jnp.bfloat16)
            dscores[h] = (probs * (dprobs[h] - delta[at, h])).astype(jnp.bfloat16)
        at, kb, _ = unlinked(chunks[i + 2], rows)
        krows = pl.ds((kb % 2) * BLOCK, BLOCK)
        for h in range(heads):
            products[h] = dot_t(kv[kb // 2, h, krows, :], x[at, h, :rows])
            dprobs[h] = dot_t(kv[kb // 2, heads + h, krows, :], x[at, h, rows : 2 * rows])
        return 0

    lax.fori_loop(0, count, body, 0)


def specs(smem, vmem, hbm):
    return (
        [pl.BlockSpec(memory_space=pltpu.SMEM)] * smem
        + [pl.BlockSpec(memory_space=pltpu.VMEM)] * vmem
        + [pl.BlockSpec(memory_space=pl.ANY)] * hbm
    )


def queries_part(near, where, span, mask, x, kv):
    heads, tall, width = x[0].shape
    rows = kv[0].shape[1]
    n = len(near)
    f32, bf16 = jnp.float32, jnp.bfloat16
    return pl.pallas_call(
        functools.partial(queries_kernel, near),
        out_shape=(
            jax.ShapeDtypeStruct((n, heads, width, rows), f32),
            jax.ShapeDtypeStruct((n, heads, rows), f32),
        ),
        in_specs=specs(3, 0, n + 4),
        out_specs=(pl.BlockSpec(memory_space=pltpu.VMEM),) * 2,
        scratch_shapes=[
            pltpu.VMEM((n, heads, tall, width), bf16),
            pltpu.VMEM((4, 2 * heads, rows, width), bf16),
            pltpu.VMEM((8, heads, width, BLOCK), bf16),
            pltpu.VMEM((n, heads, 1, rows), f32),
            pltpu.VMEM((n, heads, 1, rows), f32),
            pltpu.VMEM((n, heads, 1, rows), f32),
            pltpu.VMEM((heads, 1, rows), f32),
            pltpu.VMEM((heads, BLOCK, rows), f32),
            pltpu.VMEM((heads, BLOCK, rows), f32),
            pltpu.VMEM((heads, BLOCK, rows), bf16),
            pltpu.SMEM((8 * n + 8,), jnp.int32),
            pltpu.SemaphoreType.DMA((n + 4,)),
        ],
        compiler_params=pltpu.CompilerParams(vmem_limit_bytes=VMEM_BYTES),
        cost_estimate=pl.CostEstimate(
            flops=n * 10**9, bytes_accessed=n * 2 * 10**6, transcendentals=n * 10**6
        ),
        name="queries_part",
    )(where, span, mask, *x, *kv)


def keys_part(keys, where, span, mask, lse, x, kv):
    heads, tall, width = x[0].shape
    rows = kv[0].shape[1]
    n, m = len(x), len(keys)
    f32, bf16 = jnp.float32, jnp.bfloat16
    return pl.pallas_call(
        functools.partial(keys_kernel, keys),
        out_shape=jax.ShapeDtypeStruct((m, 2 * heads, rows, width), f32),
        in_specs=specs(3, 1, n + m),
        out_specs=pl.BlockSpec(memory_space=pltpu.VMEM),
        scratch_shapes=[
            pltpu.VMEM((n, heads, tall, width), bf16),
            pltpu.VMEM((m, 2 * heads, rows, width), bf16),
            pltpu.VMEM((n, heads, 1, rows), f32),
            pltpu.VMEM((n, heads, 1, rows), f32),
            pltpu.VMEM((heads, BLOCK, rows), f32),
            pltpu.VMEM((heads, BLOCK, rows), f32),
            pltpu.VMEM((heads, BLOCK, rows), bf16),
            pltpu.VMEM((heads, BLOCK, rows), bf16),
            pltpu.SMEM((2 * m * n + 8,), jnp.int32),
            pltpu.SemaphoreType.DMA((n + m,)),
        ],
        compiler_params=pltpu.CompilerParams(vmem_limit_bytes=VMEM_BYTES),
        cost_estimate=pl.CostEstimate(
            flops=m * 2 * 10**9, bytes_accessed=m * 3 * 10**6, transcendentals=m * 10**6
        ),
        name="keys_part",
    )(where, span, mask, lse, *x, *[kv[s] for s in keys])


def add_logs(a, b):
    top = jnp.maximum(a, b)
    return top + jnp.log2(jnp.exp2(a - top) + jnp.exp2(b - top))


def local(queries, keys, values, forward_out, out_grad, span_order, block_mask):
    rows, heads, width = queries.shape
    bf16, f32 = jnp.bfloat16, jnp.float32
    inner = lax.axis_size("inner")
    zs = inner // 2
    at = lax.axis_index("inner")
    where = jnp.stack([at // 2, at % 2, lax.axis_index("outer")]).astype(jnp.int32)

    def along(x, by):
        return lax.ppermute(x, "inner", [(i, (i + 2 * by) % inner) for i in range(inner)])

    def other_core(x):
        return lax.ppermute(x, "inner", [(i, i ^ 1) for i in range(inner)])

    def other_outer(x):
        return lax.ppermute(x, "outer", [(0, 1), (1, 0)])

    kv0 = jnp.concatenate([keys.transpose(1, 0, 2), values.transpose(1, 0, 2)], axis=0)
    delta = jnp.sum(out_grad.astype(f32) * forward_out.astype(f32), axis=2).T
    rest, terms = delta, []
    for _ in range(3):
        term = lax.reduce_precision(rest, 8, 7)
        terms.append(term.astype(bf16))
        rest = rest - term
    terms = jnp.stack(terms, axis=1).reshape(heads, 3 * rows // BLOCK, BLOCK)
    terms = jnp.pad(terms, ((0, 0), (0, 16 - terms.shape[1]), (0, 0)))
    x0 = jnp.concatenate([queries.transpose(1, 0, 2), out_grad.transpose(1, 0, 2), terms], axis=1)

    kv1 = other_outer(kv0)
    kv = [kv0, kv1, other_core(kv0), other_core(kv1)]

    half = zs // 2
    x, dq, logs = [x0] + [None] * (zs - 1), [None] * zs, [None] * zs
    for step in range(1, half + 1):
        x[zs - step] = along(x[(zs - step + 1) % zs], 1)
        if step < half:
            x[step] = along(x[step - 1], -1)

    def work(near):
        part, log = queries_part(near, where, span_order, block_mask, [x[r] for r in near], kv)
        for i, r in enumerate(near):
            dq[r], logs[r] = part[i], log[i]

    work((0, 1, zs - 1))
    for step in range(2, half):
        work((step, zs - step))
    work((half,))

    mine = jnp.stack(logs)
    lse = mine
    for d in (1, 2, 4):
        lse = add_logs(lse, jnp.roll(along(lse, -d), d, axis=0))
    share = jnp.exp2(mine - lse)[:, :, None, :]

    down = up = None
    for step in range(half):
        part = dq[half + step] * share[half + step]
        down = along((part if down is None else part + down.astype(f32)).astype(bf16), -1)
        if step >= 1:
            part = dq[half - step] * share[half - step]
            up = along((part if up is None else part + up.astype(f32)).astype(bf16), 1)
    total = dq[0] * share[0] + down.astype(f32) + up.astype(f32)
    grad_query = total.astype(bf16).transpose(2, 0, 1)

    theirs = other_core(keys_part((2, 3), where, span_order, block_mask, lse, x, kv).astype(bf16))
    dkv = keys_part((0, 1), where, span_order, block_mask, lse, x, kv) + theirs.astype(f32)
    dkv = dkv[0] + other_outer(dkv[1].astype(bf16)).astype(f32)
    grad_key = (dkv[:heads] * (1.0 / math.sqrt(width))).astype(bf16).transpose(1, 0, 2)
    return grad_query, grad_key, dkv[heads:].astype(bf16).transpose(1, 0, 2)


def solution(mesh):
    split = P(("inner", "outer"), "head", None)
    return jax.shard_map(
        local,
        mesh=mesh,
        in_specs=(split,) * 5 + (P(), P()),
        out_specs=(split,) * 3,
        check_vma=False,
    )
```

```python
import functools
import math

import jax
import jax.numpy as jnp
from jax import lax
from jax.experimental import pallas as pl
from jax.experimental.pallas import tpu as pltpu
from jax.sharding import PartitionSpec as P

BLOCK = 128
EMPTY = -1e30
VMEM_BYTES = 24 * 1024 * 1024
ZS = 8
LIST = 128


def dot_t(a, b):
    return lax.dot_general(a, b, (((1,), (1,)), ((), ())), preferred_element_type=jnp.float32)


def lists_kernel(plans, where, span, mask, chunks):
    z, core, outer = where[0], where[1], where[2]
    for p, (near, keys, many) in enumerate(plans):
        base = p * LIST
        columns = []
        for s in keys:
            piece = z * 4 + (core ^ (s // 2)) * 2 + (outer ^ (s % 2))
            for half in range(2):
                columns.append(span[piece] * 2 + half)
        for i in range(2 * many):
            chunks[base + i] = 0
        count = jnp.int32(2 * many)
        for slot, r in enumerate(near):
            row = span[lax.rem(z + r, ZS) * 4 + core * 2 + outer] * 2
            for kb in range(len(columns)):
                halves = mask[row, columns[kb]] + 2 * mask[row + 1, columns[kb]]
                chunks[base + count] = halves * 64 + slot * 8 + kb
                count = count + jnp.minimum(halves, 1)
        for i in range(3 * many - 1):
            chunks[base + count + i] = 0
        chunks[base + LIST - 1] = (count + many - 1) // many


def lists(plans, where, span, mask):
    return pl.pallas_call(
        functools.partial(lists_kernel, plans),
        out_shape=jax.ShapeDtypeStruct((len(plans) * LIST,), jnp.int32),
        in_specs=specs(3, 0, 0),
        out_specs=pl.BlockSpec(memory_space=pltpu.SMEM),
        name="lists",
    )(where, span, mask)


def unlinked(chunk, rows):
    first = lax.broadcasted_iota(jnp.int32, (1, rows), 1) < BLOCK
    halves = chunk // 64
    return (chunk // 8) % 8, chunk % 8, jnp.where(first, halves % 2, halves // 2) == 0


def gather(refs, into):
    for i, ref in enumerate(refs):
        into[i] = ref[...]


def zero(*refs):
    for ref in refs:
        ref[...] = jnp.zeros_like(ref)


def set_delta(x, delta, rows):
    for i in range(x.shape[0]):
        for h in range(x.shape[1]):
            parts = x[i, h, 2 * rows :, :].astype(jnp.float32)
            parts = parts[0:2] + parts[2:4] + parts[4:6]
            delta[i, h] = jnp.concatenate([parts[0:1], parts[1:2]], axis=1)


def queries_kernel(plan, n, chunks, *refs):
    x_in, kv_in = refs[:n], refs[n : n + 4]
    dq, lse = refs[n + 4], refs[n + 5]
    x, kv, kt, delta, top, total, decay, products, dprobs, dscores = refs[n + 6 :]
    heads, rows, width = kv.shape[1] // 2, kv.shape[2], kv.shape[3]
    gather(x_in, x)
    gather(kv_in, kv)
    scale = 1.0 / math.sqrt(width)
    factor = math.log2(math.e) * scale
    zero(dq, total, products, dprobs, dscores)
    top[...] = jnp.full_like(top, EMPTY)
    decay[...] = jnp.ones_like(decay)
    base = plan * LIST
    for s in range(4):
        for h in range(heads):
            for half in range(2):
                kt[s * 2 + half, h] = kv[s, h, half * BLOCK : (half + 1) * BLOCK, :].T
    set_delta(x, delta, rows)

    def body(i, _):
        at, kb, _ = unlinked(chunks[base + i], rows)
        for h in range(heads):
            dq[at, h] = dq[at, h] * decay[h] + jnp.dot(
                kt[kb, h], dscores[h], preferred_element_type=jnp.float32
            )
        at, kb, off = unlinked(chunks[base + i + 1], rows)
        for h in range(heads):
            scores = products[h] * factor
            old = top[at, h]
            new = jnp.where(off, old, jnp.maximum(old, jnp.max(scores, axis=0, keepdims=True)))
            probs = jnp.exp2(scores - jnp.where(off, -EMPTY, new))
            decay[h] = jnp.exp2(old - new)
            total[at, h] = total[at, h] * decay[h] + jnp.sum(probs, axis=0, keepdims=True)
            top[at, h] = new
            dscores[h] = (probs * (dprobs[h] - delta[at, h])).astype(jnp.bfloat16)
        at, kb, _ = unlinked(chunks[base + i + 2], rows)
        for h in range(heads):
            krows = pl.ds((kb % 2) * BLOCK, BLOCK)
            products[h] = dot_t(kv[kb // 2, h, krows, :], x[at, h, :rows])
            dprobs[h] = dot_t(kv[kb // 2, heads + h, krows, :], x[at, h, rows : 2 * rows])
        return 0

    lax.fori_loop(0, chunks[base + LIST - 1], body, 0)
    for i in range(n):
        for h in range(heads):
            some = total[i, h] > 0
            safe = jnp.where(some, total[i, h], 1.0)
            lse[i, h : h + 1] = jnp.where(some, top[i, h] + jnp.log2(safe), EMPTY)
            dq[i, h] = dq[i, h] * (scale / safe)


def keys_kernel(plan, m, extra, chunks, lse, *refs):
    n = ZS
    x_in, kv_in = refs[:n], refs[n : n + m]
    refs = refs[extra:]
    dkv = refs[n + m]
    x, kv, delta, logs, products, dprobs, rounded, dscores = refs[n + m + 1 :]
    heads, rows, width = kv.shape[1] // 2, kv.shape[2], kv.shape[3]
    gather(x_in, x)
    gather(kv_in, kv)
    factor = math.log2(math.e) / math.sqrt(width)
    zero(dkv, products, dprobs, rounded, dscores)
    base = plan * LIST
    for i in range(n):
        for h in range(heads):
            logs[i, h] = lse[i, h : h + 1]
    set_delta(x, delta, rows)

    def body(i, _):
        for j in range(2):
            at, kb, _ = unlinked(chunks[base + i * 2 + j], rows)
            krows = pl.ds((kb % 2) * BLOCK, BLOCK)
            for h in range(heads):
                dkv[kb // 2, heads + h, krows, :] += jnp.dot(
                    rounded[j, h], x[at, h, rows : 2 * rows], preferred_element_type=jnp.float32
                )
                dkv[kb // 2, h, krows, :] += jnp.dot(
                    dscores[j, h], x[at, h, :rows], preferred_element_type=jnp.float32
                )
        for j in range(2):
            at, kb, off = unlinked(chunks[base + (i + 1) * 2 + j], rows)
            for h in range(heads):
                probs = jnp.exp2(products[j, h] * factor - jnp.where(off, -EMPTY, logs[at, h]))
                rounded[j, h] = probs.astype(jnp.bfloat16)
                dscores[j, h] = (probs * (dprobs[j, h] - delta[at, h])).astype(jnp.bfloat16)
        for j in range(2):
            at, kb, _ = unlinked(chunks[base + (i + 2) * 2 + j], rows)
            krows = pl.ds((kb % 2) * BLOCK, BLOCK)
            for h in range(heads):
                products[j, h] = dot_t(kv[kb // 2, h, krows, :], x[at, h, :rows])
                dprobs[j, h] = dot_t(kv[kb // 2, heads + h, krows, :], x[at, h, rows : 2 * rows])
        return 0

    lax.fori_loop(0, chunks[base + LIST - 1], body, 0)


def specs(smem, vmem, hbm):
    return (
        [pl.BlockSpec(memory_space=pltpu.SMEM)] * smem
        + [pl.BlockSpec(memory_space=pltpu.VMEM)] * vmem
        + [pl.BlockSpec(memory_space=pl.ANY)] * hbm
    )


def queries_part(plan, chunks, x, kv):
    heads, tall, width = x[0].shape
    rows = kv[0].shape[1]
    n = len(x)
    f32, bf16 = jnp.float32, jnp.bfloat16
    return pl.pallas_call(
        functools.partial(queries_kernel, plan, n),
        out_shape=(
            jax.ShapeDtypeStruct((n, heads, width, rows), f32),
            jax.ShapeDtypeStruct((n, heads, rows), f32),
        ),
        in_specs=specs(1, n + 4, 0),
        out_specs=(pl.BlockSpec(memory_space=pltpu.VMEM),) * 2,
        scratch_shapes=[
            pltpu.VMEM((n, heads, tall, width), bf16),
            pltpu.VMEM((4, 2 * heads, rows, width), bf16),
            pltpu.VMEM((8, heads, width, BLOCK), bf16),
            pltpu.VMEM((n, heads, 1, rows), f32),
            pltpu.VMEM((n, heads, 1, rows), f32),
            pltpu.VMEM((n, heads, 1, rows), f32),
            pltpu.VMEM((heads, 1, rows), f32),
            pltpu.VMEM((heads, BLOCK, rows), f32),
            pltpu.VMEM((heads, BLOCK, rows), f32),
            pltpu.VMEM((heads, BLOCK, rows), bf16),
        ],
        compiler_params=pltpu.CompilerParams(vmem_limit_bytes=VMEM_BYTES),
        cost_estimate=pl.CostEstimate(
            flops=n * 10**9, bytes_accessed=n * 2 * 10**6, transcendentals=n * 10**6
        ),
        name="queries_part",
    )(chunks, *x, *kv)


def keys_part(plan, chunks, lse, x, kv, after):
    heads, tall, width = x[0].shape
    rows = kv[0].shape[1]
    n, m = len(x), len(kv)
    f32, bf16 = jnp.float32, jnp.bfloat16
    return pl.pallas_call(
        functools.partial(keys_kernel, plan, m, len(after)),
        out_shape=jax.ShapeDtypeStruct((m, 2 * heads, rows, width), f32),
        in_specs=specs(1, 1 + n + m, len(after)),
        out_specs=pl.BlockSpec(memory_space=pltpu.VMEM),
        scratch_shapes=[
            pltpu.VMEM((n, heads, tall, width), bf16),
            pltpu.VMEM((m, 2 * heads, rows, width), bf16),
            pltpu.VMEM((n, heads, 1, rows), f32),
            pltpu.VMEM((n, heads, 1, rows), f32),
            pltpu.VMEM((2, heads, BLOCK, rows), f32),
            pltpu.VMEM((2, heads, BLOCK, rows), f32),
            pltpu.VMEM((2, heads, BLOCK, rows), bf16),
            pltpu.VMEM((2, heads, BLOCK, rows), bf16),
        ],
        compiler_params=pltpu.CompilerParams(vmem_limit_bytes=VMEM_BYTES),
        cost_estimate=pl.CostEstimate(
            flops=m * 2 * 10**9, bytes_accessed=m * 3 * 10**6, transcendentals=m * 10**6
        ),
        name="keys_part",
    )(chunks, lse, *x, *kv, *after)


def add_logs(a, b):
    top = jnp.maximum(a, b)
    return top + jnp.log2(jnp.exp2(a - top) + jnp.exp2(b - top))


def local(queries, keys, values, forward_out, out_grad, span_order, block_mask):
    rows, heads, width = queries.shape
    bf16, f32 = jnp.bfloat16, jnp.float32
    inner = lax.axis_size("inner")
    zs = inner // 2
    at = lax.axis_index("inner")
    where = jnp.stack([at // 2, at % 2, lax.axis_index("outer")]).astype(jnp.int32)

    def along(x, by):
        return lax.ppermute(x, "inner", [(i, (i + 2 * by) % inner) for i in range(inner)])

    def other_core(x):
        return lax.ppermute(x, "inner", [(i, i ^ 1) for i in range(inner)])

    def other_outer(x):
        return lax.ppermute(x, "outer", [(0, 1), (1, 0)])

    delta = jnp.sum(out_grad.astype(f32) * forward_out.astype(f32), axis=2).T
    rest, terms = delta, []
    for _ in range(3):
        term = lax.reduce_precision(rest, 8, 7)
        terms.append(term.astype(bf16))
        rest = rest - term
    terms = jnp.stack(terms, axis=1).reshape(heads, 3 * rows // BLOCK, BLOCK)
    terms = jnp.pad(terms, ((0, 0), (0, 16 - terms.shape[1]), (0, 0)))
    x0 = jnp.concatenate([queries.transpose(1, 0, 2), out_grad.transpose(1, 0, 2), terms], axis=1)

    keys, values, x0 = lax.optimization_barrier((keys, values, x0))
    kv0 = jnp.concatenate([keys.transpose(1, 0, 2), values.transpose(1, 0, 2)], axis=0)
    kv1 = other_outer(kv0)
    kv = [kv0, kv1, other_core(kv0), other_core(kv1)]

    half = zs // 2
    x, dq, logs = [x0] + [None] * (zs - 1), [None] * zs, [None] * zs
    for step in range(1, half + 1):
        x[zs - step] = along(x[(zs - step + 1) % zs], 1)
        if step < half:
            x[step] = along(x[step - 1], -1)

    groups = [(0, 1, zs - 1)] + [(step, zs - step) for step in range(2, half)] + [(half,)]
    turns = [(1, 3), (2,), (0,)]
    plans = [(near, range(4), 1) for near in groups] + [(range(zs), pieces, 2) for pieces in turns]
    chunks = lists(plans, where, span_order, block_mask)
    for plan, near in enumerate(groups):
        part, log = queries_part(plan, chunks, [x[r] for r in near], kv)
        for i, r in enumerate(near):
            dq[r], logs[r] = part[i], log[i]

    mine = jnp.stack(logs)
    lse = mine
    for d in (1, 2, 4):
        lse = add_logs(lse, jnp.roll(along(lse, -d), d, axis=0))
    share = jnp.exp2(mine - lse)[:, :, None, :]

    down = up = None
    sums = []
    for step in range(half):
        part = dq[half + step] * share[half + step]
        sums.append([(part if down is None else part + down.astype(f32)).astype(bf16)])
        down = along(sums[step][0], -1)
        if step >= 1:
            part = dq[half - step] * share[half - step]
            sums[step].append((part if up is None else part + up.astype(f32)).astype(bf16))
            up = along(sums[step][1], 1)
    total = dq[0] * share[0] + down.astype(f32) + up.astype(f32)
    grad_query = total.astype(bf16).transpose(2, 0, 1)

    def keys_of(turn, after):
        return keys_part(len(groups) + turn, chunks, lse, x, [kv[s] for s in turns[turn]], after)

    away = keys_of(0, sums[0])
    away = (away[0] + other_core(away[1].astype(bf16)).astype(f32)).astype(bf16)
    next_core = keys_of(1, [away] + sums[2])[0].astype(bf16)
    own = keys_of(2, [next_core] + sums[3])[0]
    dkv = own + other_core(next_core).astype(f32) + other_outer(away).astype(f32)
    grad_key = (dkv[:heads] * (1.0 / math.sqrt(width))).astype(bf16).transpose(1, 0, 2)
    return grad_query, grad_key, dkv[heads:].astype(bf16).transpose(1, 0, 2)


def solution(mesh):
    split = P(("inner", "outer"), "head", None)
    return jax.shard_map(
        local,
        mesh=mesh,
        in_specs=(split,) * 5 + (P(), P()),
        out_specs=(split,) * 3,
        check_vma=False,
    )
```

```python
import functools
import math

import jax
import jax.numpy as jnp
from jax import lax
from jax.experimental import pallas as pl
from jax.experimental.pallas import tpu as pltpu
from jax.sharding import PartitionSpec as P

BLOCK = 128
EMPTY = -1e30
VMEM_BYTES = 20 * 1024 * 1024
ZS = 8
LIST = 128


def dot_t(a, b):
    return lax.dot_general(a, b, (((1,), (1,)), ((), ())), preferred_element_type=jnp.float32)


def lists_kernel(plans, where, span, mask, chunks):
    z, core, outer = where[0], where[1], where[2]
    for p, (near, keys, many) in enumerate(plans):
        base = p * LIST
        columns = []
        for s in keys:
            piece = z * 4 + (core ^ (s // 2)) * 2 + (outer ^ (s % 2))
            for half in range(2):
                columns.append(span[piece] * 2 + half)
        for i in range(2 * many):
            chunks[base + i] = 0
        count = jnp.int32(2 * many)
        for slot, r in enumerate(near):
            row = span[lax.rem(z + r, ZS) * 4 + core * 2 + outer] * 2
            for kb in range(len(columns)):
                halves = mask[row, columns[kb]] + 2 * mask[row + 1, columns[kb]]
                chunks[base + count] = halves * 64 + slot * 8 + kb
                count = count + jnp.minimum(halves, 1)
        for i in range(3 * many - 1):
            chunks[base + count + i] = 0
        chunks[base + LIST - 1] = (count + many - 1) // many


def lists(plans, where, span, mask):
    return pl.pallas_call(
        functools.partial(lists_kernel, plans),
        out_shape=jax.ShapeDtypeStruct((len(plans) * LIST,), jnp.int32),
        in_specs=specs(3, 0, 0),
        out_specs=pl.BlockSpec(memory_space=pltpu.SMEM),
        compiler_params=pltpu.CompilerParams(vmem_limit_bytes=2**20),
        name="lists",
    )(where, span, mask)


def unlinked(chunk, rows):
    first = lax.broadcasted_iota(jnp.int32, (1, rows), 1) < BLOCK
    halves = chunk // 64
    return (chunk // 8) % 8, chunk % 8, jnp.where(first, halves % 2, halves // 2) == 0


def gather(refs, into):
    piece = at = 0
    for ref in refs:
        into[piece, :, at : at + ref.shape[1]] = ref[...]
        at += ref.shape[1]
        if at == into.shape[2]:
            piece, at = piece + 1, 0


def zero(*refs):
    for ref in refs:
        ref[...] = jnp.zeros_like(ref)


def set_delta(x, delta, rows):
    for i in range(x.shape[0]):
        for h in range(x.shape[1]):
            parts = x[i, h, 2 * rows :, :].astype(jnp.float32)
            parts = parts[0:2] + parts[2:4] + parts[4:6]
            delta[i, h] = jnp.concatenate([parts[0:1], parts[1:2]], axis=1)


def queries_kernel(plan, n, chunks, *refs):
    p = len(refs) - 16
    x_in, kv_in = refs[:p], refs[p : p + 4]
    dq, lse = refs[p + 4], refs[p + 5]
    x, kv, kt, delta, top, total, decay, products, dprobs, dscores = refs[p + 6 :]
    heads, rows, width = kv.shape[1] // 2, kv.shape[2], kv.shape[3]
    gather(x_in, x)
    gather(kv_in, kv)
    scale = 1.0 / math.sqrt(width)
    factor = math.log2(math.e) * scale
    zero(dq, total, products, dprobs, dscores)
    top[...] = jnp.full_like(top, EMPTY)
    decay[...] = jnp.ones_like(decay)
    base = plan * LIST
    for s in range(4):
        for h in range(heads):
            for half in range(2):
                kt[s * 2 + half, h] = kv[s, h, half * BLOCK : (half + 1) * BLOCK, :].T
    set_delta(x, delta, rows)

    def body(i, _):
        at, kb, _ = unlinked(chunks[base + i], rows)
        for h in range(heads):
            dq[at, h] = dq[at, h] * decay[h] + jnp.dot(
                kt[kb, h], dscores[h], preferred_element_type=jnp.float32
            )
        at, kb, off = unlinked(chunks[base + i + 1], rows)
        for h in range(heads):
            scores = products[h] * factor
            old = top[at, h]
            new = jnp.where(off, old, jnp.maximum(old, jnp.max(scores, axis=0, keepdims=True)))
            probs = jnp.exp2(scores - jnp.where(off, -EMPTY, new))
            decay[h] = jnp.exp2(old - new)
            total[at, h] = total[at, h] * decay[h] + jnp.sum(probs, axis=0, keepdims=True)
            top[at, h] = new
            dscores[h] = (probs * (dprobs[h] - delta[at, h])).astype(jnp.bfloat16)
        at, kb, _ = unlinked(chunks[base + i + 2], rows)
        for h in range(heads):
            krows = pl.ds((kb % 2) * BLOCK, BLOCK)
            products[h] = dot_t(kv[kb // 2, h, krows, :], x[at, h, :rows])
            dprobs[h] = dot_t(kv[kb // 2, heads + h, krows, :], x[at, h, rows : 2 * rows])
        return 0

    lax.fori_loop(0, chunks[base + LIST - 1], body, 0)
    for i in range(n):
        for h in range(heads):
            some = total[i, h] > 0
            safe = jnp.where(some, total[i, h], 1.0)
            lse[i, h : h + 1] = jnp.where(some, top[i, h] + jnp.log2(safe), EMPTY)
            dq[i, h] = dq[i, h] * (scale / safe)


def keys_kernel(plan, m, extra, chunks, lse, *refs):
    n = ZS
    p = len(refs) - extra - m - 9
    x_in, kv_in = refs[:p], refs[p : p + m]
    refs = refs[p + m + extra :]
    dkv = refs[0]
    x, kv, delta, logs, products, dprobs, rounded, dscores = refs[1:]
    heads, rows, width = kv.shape[1] // 2, kv.shape[2], kv.shape[3]
    gather(x_in, x)
    gather(kv_in, kv)
    factor = math.log2(math.e) / math.sqrt(width)
    zero(dkv, products, dprobs, rounded, dscores)
    base = plan * LIST
    for i in range(n):
        for h in range(heads):
            logs[i, h] = lse[i, h : h + 1]
    set_delta(x, delta, rows)

    def body(i, _):
        for j in range(2):
            at, kb, _ = unlinked(chunks[base + i * 2 + j], rows)
            krows = pl.ds((kb % 2) * BLOCK, BLOCK)
            for h in range(heads):
                dkv[kb // 2, heads + h, krows, :] += jnp.dot(
                    rounded[j, h], x[at, h, rows : 2 * rows], preferred_element_type=jnp.float32
                )
                dkv[kb // 2, h, krows, :] += jnp.dot(
                    dscores[j, h], x[at, h, :rows], preferred_element_type=jnp.float32
                )
        for j in range(2):
            at, kb, off = unlinked(chunks[base + (i + 1) * 2 + j], rows)
            for h in range(heads):
                probs = jnp.exp2(products[j, h] * factor - jnp.where(off, -EMPTY, logs[at, h]))
                rounded[j, h] = probs.astype(jnp.bfloat16)
                dscores[j, h] = (probs * (dprobs[j, h] - delta[at, h])).astype(jnp.bfloat16)
        for j in range(2):
            at, kb, _ = unlinked(chunks[base + (i + 2) * 2 + j], rows)
            krows = pl.ds((kb % 2) * BLOCK, BLOCK)
            for h in range(heads):
                products[j, h] = dot_t(kv[kb // 2, h, krows, :], x[at, h, :rows])
                dprobs[j, h] = dot_t(kv[kb // 2, heads + h, krows, :], x[at, h, rows : 2 * rows])
        return 0

    lax.fori_loop(0, chunks[base + LIST - 1], body, 0)


def specs(smem, vmem, hbm):
    return (
        [pl.BlockSpec(memory_space=pltpu.SMEM)] * smem
        + [pl.BlockSpec(memory_space=pltpu.VMEM)] * vmem
        + [pl.BlockSpec(memory_space=pl.ANY)] * hbm
    )


def queries_part(plan, chunks, x, kv):
    heads, rows, width = kv[0].shape[0] // 2, kv[0].shape[1], kv[0].shape[2]
    tall = 2 * rows + 16
    n = len(x)
    x = [part for piece in x for part in piece]
    p = len(x)
    f32, bf16 = jnp.float32, jnp.bfloat16
    return pl.pallas_call(
        functools.partial(queries_kernel, plan, n),
        out_shape=(
            jax.ShapeDtypeStruct((n, heads, width, rows), f32),
            jax.ShapeDtypeStruct((n, heads, rows), f32),
        ),
        in_specs=specs(1, p + 4, 0),
        out_specs=(pl.BlockSpec(memory_space=pltpu.VMEM),) * 2,
        scratch_shapes=[
            pltpu.VMEM((n, heads, tall, width), bf16),
            pltpu.VMEM((4, 2 * heads, rows, width), bf16),
            pltpu.VMEM((8, heads, width, BLOCK), bf16),
            pltpu.VMEM((n, heads, 1, rows), f32),
            pltpu.VMEM((n, heads, 1, rows), f32),
            pltpu.VMEM((n, heads, 1, rows), f32),
            pltpu.VMEM((heads, 1, rows), f32),
            pltpu.VMEM((heads, BLOCK, rows), f32),
            pltpu.VMEM((heads, BLOCK, rows), f32),
            pltpu.VMEM((heads, BLOCK, rows), bf16),
        ],
        compiler_params=pltpu.CompilerParams(vmem_limit_bytes=VMEM_BYTES),
        cost_estimate=pl.CostEstimate(
            flops=n * 10**9, bytes_accessed=n * 2 * 10**6, transcendentals=n * 10**6
        ),
        name="queries_part",
    )(chunks, *x, *kv)


def keys_part(plan, chunks, lse, x, kv, after):
    heads, rows, width = kv[0].shape[0] // 2, kv[0].shape[1], kv[0].shape[2]
    tall = 2 * rows + 16
    n, m = len(x), len(kv)
    x = [part for piece in x for part in piece]
    p = len(x)
    f32, bf16 = jnp.float32, jnp.bfloat16
    return pl.pallas_call(
        functools.partial(keys_kernel, plan, m, len(after)),
        out_shape=jax.ShapeDtypeStruct((m, 2 * heads, rows, width), f32),
        in_specs=specs(1, 1 + p + m, len(after)),
        out_specs=pl.BlockSpec(memory_space=pltpu.VMEM),
        scratch_shapes=[
            pltpu.VMEM((n, heads, tall, width), bf16),
            pltpu.VMEM((m, 2 * heads, rows, width), bf16),
            pltpu.VMEM((n, heads, 1, rows), f32),
            pltpu.VMEM((n, heads, 1, rows), f32),
            pltpu.VMEM((2, heads, BLOCK, rows), f32),
            pltpu.VMEM((2, heads, BLOCK, rows), f32),
            pltpu.VMEM((2, heads, BLOCK, rows), bf16),
            pltpu.VMEM((2, heads, BLOCK, rows), bf16),
        ],
        compiler_params=pltpu.CompilerParams(vmem_limit_bytes=VMEM_BYTES),
        cost_estimate=pl.CostEstimate(
            flops=m * 2 * 10**9, bytes_accessed=m * 3 * 10**6, transcendentals=m * 10**6
        ),
        name="keys_part",
    )(chunks, lse, *x, *kv, *after)


def add_logs(a, b):
    top = jnp.maximum(a, b)
    return top + jnp.log2(jnp.exp2(a - top) + jnp.exp2(b - top))


def terms_of(x):
    terms = []
    for _ in range(3):
        term = lax.reduce_precision(x, 8, 7)
        terms.append(term.astype(jnp.bfloat16))
        x = x - term
    return terms


def local(queries, keys, values, forward_out, out_grad, span_order, block_mask):
    rows, heads, width = queries.shape
    bf16, f32 = jnp.bfloat16, jnp.float32
    inner = lax.axis_size("inner")
    zs = inner // 2
    at = lax.axis_index("inner")
    where = jnp.stack([at // 2, at % 2, lax.axis_index("outer")]).astype(jnp.int32)

    def along(x, by):
        return lax.ppermute(x, "inner", [(i, (i + 2 * by) % inner) for i in range(inner)])

    def other_core(x):
        return lax.ppermute(x, "inner", [(i, i ^ 1) for i in range(inner)])

    def other_outer(x):
        return lax.ppermute(x, "outer", [(0, 1), (1, 0)])

    delta = jnp.sum(out_grad.astype(f32) * forward_out.astype(f32), axis=2).T
    terms = jnp.stack(terms_of(delta), axis=1).reshape(heads, 3 * rows // BLOCK, BLOCK)
    terms = jnp.pad(terms, ((0, 0), (0, 16 - terms.shape[1]), (0, 0)))
    x0 = jnp.concatenate([queries.transpose(1, 0, 2), out_grad.transpose(1, 0, 2), terms], axis=1)

    keys, values, x0 = lax.optimization_barrier((keys, values, x0))
    kv0 = jnp.concatenate([keys.transpose(1, 0, 2), values.transpose(1, 0, 2)], axis=0)
    kv1 = other_outer(kv0)
    kv = [kv0, kv1, other_core(kv0), other_core(kv1)]

    half = zs // 2
    x, dq, logs = [x0] + [None] * (zs - 1), [None] * zs, [None] * zs
    for step in range(1, half):
        x[zs - step] = along(x[(zs - step + 1) % zs], 1)
        x[step] = along(x[step - 1], -1)
    far = (along(x[half + 1][:, :rows], 1), along(x[half - 1][:, rows:], -1))
    x = [(piece,) for piece in x]
    x[half] = far

    groups = [(0, 1, zs - 1)] + [(step, zs - step) for step in range(2, half)] + [(half,)]
    turns = [(1, 3), (0, 2)]
    plans = [(near, range(4), 1) for near in groups] + [(range(zs), pieces, 2) for pieces in turns]
    chunks = lists(plans, where, span_order, block_mask)
    for plan, near in enumerate(groups):
        part, log = queries_part(plan, chunks, [x[r] for r in near], kv)
        for i, r in enumerate(near):
            dq[r], logs[r] = part[i], log[i]

    early = jnp.pad(jnp.stack(terms_of(logs[half]), axis=1), ((0, 0), (0, 13), (0, 0)))
    early = along(jnp.concatenate([dq[half].astype(bf16), early], axis=1), -1)
    early_logs = jnp.sum(early[:, width : width + 3].astype(f32), axis=1)

    mine = jnp.stack(logs)
    lse = mine
    for d in (1, 2, 4):
        if d == 4:
            lse = lse + jnp.minimum(jnp.abs(early_logs), 0.0)
        lse = add_logs(lse, jnp.roll(along(lse, -d), d, axis=0))
    share = jnp.exp2(mine - lse)[:, :, None, :]

    down = early[:, :width].astype(f32) * jnp.exp2(early_logs - lse[half + 1])[:, None, :]
    up = None
    sums = [[]]
    for step in range(1, half):
        part = dq[half + step] * share[half + step]
        sums.append([(part + down.astype(f32)).astype(bf16)])
        down = along(sums[step][0], -1)
        part = dq[half - step] * share[half - step]
        sums[step].append((part if up is None else part + up.astype(f32)).astype(bf16))
        up = along(sums[step][1], 1)
    total = dq[0] * share[0] + down.astype(f32) + up.astype(f32)
    grad_query = total.astype(bf16).transpose(2, 0, 1)

    def keys_of(turn, after):
        return keys_part(len(groups) + turn, chunks, lse, x, [kv[s] for s in turns[turn]], after)

    away = keys_of(0, sums[1])
    away = (away[0] + other_core(away[1].astype(bf16)).astype(f32)).astype(bf16)
    own = keys_of(1, [away] + sums[3])
    theirs, away = other_core(own[1].astype(bf16)), other_outer(away)
    key, value = (
        own[0, part] + theirs[part].astype(f32) + away[part].astype(f32)
        for part in (slice(0, heads), slice(heads, 2 * heads))
    )
    grad_key = (key * (1.0 / math.sqrt(width))).astype(bf16).transpose(1, 0, 2)
    return grad_query, grad_key, value.astype(bf16).transpose(1, 0, 2)


def solution(mesh):
    split = P(("inner", "outer"), "head", None)
    return jax.shard_map(
        local,
        mesh=mesh,
        in_specs=(split,) * 5 + (P(), P()),
        out_specs=(split,) * 3,
        check_vma=False,
    )
```

```python
import functools
import math

import jax
import jax.numpy as jnp
from jax import lax
from jax.experimental import pallas as pl
from jax.experimental.pallas import tpu as pltpu
from jax.sharding import PartitionSpec as P

BLOCK = 128
EMPTY = -1e30
VMEM_BYTES = 20 * 1024 * 1024
ZS = 8
LIST = 128


def dot_t(a, b):
    return lax.dot_general(a, b, (((1,), (1,)), ((), ())), preferred_element_type=jnp.float32)


def lists_kernel(plans, where, span, mask, chunks):
    z, core, outer = where[0], where[1], where[2]
    for p, (near, keys, many) in enumerate(plans):
        base = p * LIST
        columns = []
        for s in keys:
            piece = z * 4 + (core ^ (s // 2)) * 2 + (outer ^ (s % 2))
            for half in range(2):
                columns.append(span[piece] * 2 + half)
        for i in range(2 * many):
            chunks[base + i] = 0
        count = jnp.int32(2 * many)
        for slot, r in enumerate(near):
            row = span[lax.rem(z + r, ZS) * 4 + core * 2 + outer] * 2
            for kb in range(len(columns)):
                halves = mask[row, columns[kb]] + 2 * mask[row + 1, columns[kb]]
                chunks[base + count] = halves * 64 + slot * 8 + kb
                count = count + jnp.minimum(halves, 1)
        for i in range(3 * many - 1):
            chunks[base + count + i] = 0
        chunks[base + LIST - 1] = (count + many - 1) // many


def lists(plans, where, span, mask):
    return pl.pallas_call(
        functools.partial(lists_kernel, plans),
        out_shape=jax.ShapeDtypeStruct((len(plans) * LIST,), jnp.int32),
        in_specs=specs(3, 0, 0),
        out_specs=pl.BlockSpec(memory_space=pltpu.SMEM),
        compiler_params=pltpu.CompilerParams(vmem_limit_bytes=2**20),
        name="lists",
    )(where, span, mask)


def unlinked(chunk, rows):
    first = lax.broadcasted_iota(jnp.int32, (1, rows), 1) < BLOCK
    halves = chunk // 64
    return (chunk // 8) % 8, chunk % 8, jnp.where(first, halves % 2, halves // 2) == 0


def gather(refs, into):
    piece = at = 0
    for ref in refs:
        into[piece, :, at : at + ref.shape[1]] = ref[...]
        at += ref.shape[1]
        if at == into.shape[2]:
            piece, at = piece + 1, 0


def zero(*refs):
    for ref in refs:
        ref[...] = jnp.zeros_like(ref)


def set_delta(x, delta, rows):
    for i in range(x.shape[0]):
        for h in range(x.shape[1]):
            parts = x[i, h, 2 * rows :, :].astype(jnp.float32)
            parts = parts[0:2] + parts[2:4] + parts[4:6]
            delta[i, h] = jnp.concatenate([parts[0:1], parts[1:2]], axis=1)


def queries_kernel(plan, n, chunks, *refs):
    p = len(refs) - 16
    x_in, kv_in = refs[:p], refs[p : p + 4]
    dq, lse = refs[p + 4], refs[p + 5]
    x, kv, kt, delta, top, total, decay, products, dprobs, dscores = refs[p + 6 :]
    heads, rows, width = kv.shape[1] // 2, kv.shape[2], kv.shape[3]
    gather(x_in, x)
    gather(kv_in, kv)
    scale = 1.0 / math.sqrt(width)
    factor = math.log2(math.e) * scale
    zero(dq, total, products, dprobs, dscores)
    top[...] = jnp.full_like(top, EMPTY)
    decay[...] = jnp.ones_like(decay)
    base = plan * LIST
    for s in range(4):
        for h in range(heads):
            for half in range(2):
                kt[s * 2 + half, h] = kv[s, h, half * BLOCK : (half + 1) * BLOCK, :].T
    set_delta(x, delta, rows)

    def body(i, _):
        at, kb, _ = unlinked(chunks[base + i], rows)
        for h in range(heads):
            dq[at, h] = dq[at, h] * decay[h] + jnp.dot(
                kt[kb, h], dscores[h], preferred_element_type=jnp.float32
            )
        at, kb, off = unlinked(chunks[base + i + 1], rows)
        for h in range(heads):
            scores = products[h] * factor
            old = top[at, h]
            new = jnp.where(off, old, jnp.maximum(old, jnp.max(scores, axis=0, keepdims=True)))
            probs = jnp.exp2(scores - jnp.where(off, -EMPTY, new))
            decay[h] = jnp.exp2(old - new)
            total[at, h] = total[at, h] * decay[h] + jnp.sum(probs, axis=0, keepdims=True)
            top[at, h] = new
            dscores[h] = (probs * (dprobs[h] - delta[at, h])).astype(jnp.bfloat16)
        at, kb, _ = unlinked(chunks[base + i + 2], rows)
        for h in range(heads):
            krows = pl.ds((kb % 2) * BLOCK, BLOCK)
            products[h] = dot_t(kv[kb // 2, h, krows, :], x[at, h, :rows])
            dprobs[h] = dot_t(kv[kb // 2, heads + h, krows, :], x[at, h, rows : 2 * rows])
        return 0

    lax.fori_loop(0, chunks[base + LIST - 1], body, 0)
    for i in range(n):
        for h in range(heads):
            some = total[i, h] > 0
            safe = jnp.where(some, total[i, h], 1.0)
            lse[i, h : h + 1] = jnp.where(some, top[i, h] + jnp.log2(safe), EMPTY)
            dq[i, h] = dq[i, h] * (scale / safe)


def keys_kernel(plan, m, extra, chunks, lse, *refs):
    n = ZS
    p = len(refs) - extra - m - 9
    x_in, kv_in = refs[:p], refs[p : p + m]
    refs = refs[p + m + extra :]
    dkv = refs[0]
    x, kv, delta, logs, products, dprobs, rounded, dscores = refs[1:]
    heads, rows, width = kv.shape[1] // 2, kv.shape[2], kv.shape[3]
    gather(x_in, x)
    gather(kv_in, kv)
    factor = math.log2(math.e) / math.sqrt(width)
    zero(dkv, products, dprobs, rounded, dscores)
    base = plan * LIST
    for i in range(n):
        for h in range(heads):
            logs[i, h] = lse[i, h : h + 1]
    set_delta(x, delta, rows)

    def body(i, _):
        for j in range(2):
            at, kb, _ = unlinked(chunks[base + i * 2 + j], rows)
            krows = pl.ds((kb % 2) * BLOCK, BLOCK)
            for h in range(heads):
                dkv[kb // 2, heads + h, krows, :] += jnp.dot(
                    rounded[j, h], x[at, h, rows : 2 * rows], preferred_element_type=jnp.float32
                )
                dkv[kb // 2, h, krows, :] += jnp.dot(
                    dscores[j, h], x[at, h, :rows], preferred_element_type=jnp.float32
                )
        for j in range(2):
            at, kb, off = unlinked(chunks[base + (i + 1) * 2 + j], rows)
            for h in range(heads):
                probs = jnp.exp2(products[j, h] * factor - jnp.where(off, -EMPTY, logs[at, h]))
                rounded[j, h] = probs.astype(jnp.bfloat16)
                dscores[j, h] = (probs * (dprobs[j, h] - delta[at, h])).astype(jnp.bfloat16)
        for j in range(2):
            at, kb, _ = unlinked(chunks[base + (i + 2) * 2 + j], rows)
            krows = pl.ds((kb % 2) * BLOCK, BLOCK)
            for h in range(heads):
                products[j, h] = dot_t(kv[kb // 2, h, krows, :], x[at, h, :rows])
                dprobs[j, h] = dot_t(kv[kb // 2, heads + h, krows, :], x[at, h, rows : 2 * rows])
        return 0

    lax.fori_loop(0, chunks[base + LIST - 1], body, 0)


def specs(smem, vmem, hbm):
    return (
        [pl.BlockSpec(memory_space=pltpu.SMEM)] * smem
        + [pl.BlockSpec(memory_space=pltpu.VMEM)] * vmem
        + [pl.BlockSpec(memory_space=pl.ANY)] * hbm
    )


def queries_part(plan, chunks, x, kv):
    heads, rows, width = kv[0].shape[0] // 2, kv[0].shape[1], kv[0].shape[2]
    tall = 2 * rows + 16
    n = len(x)
    x = [part for piece in x for part in piece]
    p = len(x)
    f32, bf16 = jnp.float32, jnp.bfloat16
    return pl.pallas_call(
        functools.partial(queries_kernel, plan, n),
        out_shape=(
            jax.ShapeDtypeStruct((n, heads, width, rows), f32),
            jax.ShapeDtypeStruct((n, heads, rows), f32),
        ),
        in_specs=specs(1, p + 4, 0),
        out_specs=(pl.BlockSpec(memory_space=pltpu.VMEM),) * 2,
        scratch_shapes=[
            pltpu.VMEM((n, heads, tall, width), bf16),
            pltpu.VMEM((4, 2 * heads, rows, width), bf16),
            pltpu.VMEM((8, heads, width, BLOCK), bf16),
            pltpu.VMEM((n, heads, 1, rows), f32),
            pltpu.VMEM((n, heads, 1, rows), f32),
            pltpu.VMEM((n, heads, 1, rows), f32),
            pltpu.VMEM((heads, 1, rows), f32),
            pltpu.VMEM((heads, BLOCK, rows), f32),
            pltpu.VMEM((heads, BLOCK, rows), f32),
            pltpu.VMEM((heads, BLOCK, rows), bf16),
        ],
        compiler_params=pltpu.CompilerParams(vmem_limit_bytes=VMEM_BYTES),
        cost_estimate=pl.CostEstimate(
            flops=n * 10**9, bytes_accessed=n * 2 * 10**6, transcendentals=n * 10**6
        ),
        name="queries_part",
    )(chunks, *x, *kv)


def keys_part(plan, chunks, lse, x, kv, after):
    heads, rows, width = kv[0].shape[0] // 2, kv[0].shape[1], kv[0].shape[2]
    tall = 2 * rows + 16
    n, m = len(x), len(kv)
    x = [part for piece in x for part in piece]
    p = len(x)
    f32, bf16 = jnp.float32, jnp.bfloat16
    return pl.pallas_call(
        functools.partial(keys_kernel, plan, m, len(after)),
        out_shape=jax.ShapeDtypeStruct((m, 2 * heads, rows, width), f32),
        in_specs=specs(1, 1 + p + m, len(after)),
        out_specs=pl.BlockSpec(memory_space=pltpu.VMEM),
        scratch_shapes=[
            pltpu.VMEM((n, heads, tall, width), bf16),
            pltpu.VMEM((m, 2 * heads, rows, width), bf16),
            pltpu.VMEM((n, heads, 1, rows), f32),
            pltpu.VMEM((n, heads, 1, rows), f32),
            pltpu.VMEM((2, heads, BLOCK, rows), f32),
            pltpu.VMEM((2, heads, BLOCK, rows), f32),
            pltpu.VMEM((2, heads, BLOCK, rows), bf16),
            pltpu.VMEM((2, heads, BLOCK, rows), bf16),
        ],
        compiler_params=pltpu.CompilerParams(vmem_limit_bytes=VMEM_BYTES),
        cost_estimate=pl.CostEstimate(
            flops=m * 2 * 10**9, bytes_accessed=m * 3 * 10**6, transcendentals=m * 10**6
        ),
        name="keys_part",
    )(chunks, lse, *x, *kv, *after)


def add_logs(a, b):
    top = jnp.maximum(a, b)
    return top + jnp.log2(jnp.exp2(a - top) + jnp.exp2(b - top))


def terms_of(x):
    terms = []
    for _ in range(3):
        term = lax.reduce_precision(x, 8, 7)
        terms.append(term.astype(jnp.bfloat16))
        x = x - term
    return terms


def local(queries, keys, values, forward_out, out_grad, span_order, block_mask):
    rows, heads, width = queries.shape
    bf16, f32 = jnp.bfloat16, jnp.float32
    inner = lax.axis_size("inner")
    zs = inner // 2
    at = lax.axis_index("inner")
    where = jnp.stack([at // 2, at % 2, lax.axis_index("outer")]).astype(jnp.int32)

    def along(x, by):
        return lax.ppermute(x, "inner", [(i, (i + 2 * by) % inner) for i in range(inner)])

    def other_core(x):
        return lax.ppermute(x, "inner", [(i, i ^ 1) for i in range(inner)])

    def other_outer(x):
        return lax.ppermute(x, "outer", [(0, 1), (1, 0)])

    delta = jnp.sum(out_grad.astype(f32) * forward_out.astype(f32), axis=2).T
    terms = jnp.stack(terms_of(delta), axis=1).reshape(heads, 3 * rows // BLOCK, BLOCK)
    terms = jnp.pad(terms, ((0, 0), (0, 16 - terms.shape[1]), (0, 0)))
    x0 = jnp.concatenate([queries.transpose(1, 0, 2), out_grad.transpose(1, 0, 2), terms], axis=1)

    keys, values, x0 = lax.optimization_barrier((keys, values, x0))
    kv0 = jnp.concatenate([keys.transpose(1, 0, 2), values.transpose(1, 0, 2)], axis=0)
    kv1 = other_outer(kv0)
    kv = [kv0, kv1, other_core(kv0), other_core(kv1)]

    half = zs // 2
    x, dq, logs = [x0] + [None] * (zs - 1), [None] * zs, [None] * zs
    for step in range(1, half):
        x[zs - step] = along(x[(zs - step + 1) % zs], 1)
        x[step] = along(x[step - 1], -1)
    far = (along(x[half + 1][:, :rows], 1), along(x[half - 1][:, rows:], -1))
    x = [(piece,) for piece in x]
    x[half] = far

    groups = [(0, 1, zs - 1)] + [(step, zs - step) for step in range(2, half)] + [(half,)]
    turns = [(1, 3), (2,), (0,)]
    plans = [(near, range(4), 1) for near in groups] + [(range(zs), pieces, 2) for pieces in turns]
    chunks = lists(plans, where, span_order, block_mask)
    for plan, near in enumerate(groups):
        part, log = queries_part(plan, chunks, [x[r] for r in near], kv)
        for i, r in enumerate(near):
            dq[r], logs[r] = part[i], log[i]

    early = jnp.pad(jnp.stack(terms_of(logs[half]), axis=1), ((0, 0), (0, 13), (0, 0)))
    early = along(jnp.concatenate([dq[half].astype(bf16), early], axis=1), -1)
    early_logs = jnp.sum(early[:, width : width + 3].astype(f32), axis=1)

    mine = jnp.stack(logs)
    lse = mine
    for d in (1, 2, 4):
        if d == 4:
            lse = lse + jnp.minimum(jnp.abs(early_logs), 0.0)
        lse = add_logs(lse, jnp.roll(along(lse, -d), d, axis=0))
    share = jnp.exp2(mine - lse)[:, :, None, :]

    down = early[:, :width].astype(f32) * jnp.exp2(early_logs - lse[half + 1])[:, None, :]
    up = None
    sums = [[]]
    for step in range(1, half):
        part = dq[half + step] * share[half + step]
        sums.append([(part + down.astype(f32)).astype(bf16)])
        down = along(sums[step][0], -1)
        part = dq[half - step] * share[half - step]
        sums[step].append((part if up is None else part + up.astype(f32)).astype(bf16))
        up = along(sums[step][1], 1)
    total = dq[0] * share[0] + down.astype(f32) + up.astype(f32)
    grad_query = total.astype(bf16).transpose(2, 0, 1)

    def keys_of(turn, after):
        return keys_part(len(groups) + turn, chunks, lse, x, [kv[s] for s in turns[turn]], after)

    away = keys_of(0, sums[1])
    away = (away[0] + other_core(away[1].astype(bf16)).astype(f32)).astype(bf16)
    theirs = keys_of(1, [away] + sums[2])[0].astype(bf16)
    away = other_outer(away)
    own = keys_of(2, [away] + sums[3])[0]
    theirs = other_core(theirs)
    key, value = (
        own[part] + theirs[part].astype(f32) + away[part].astype(f32)
        for part in (slice(0, heads), slice(heads, 2 * heads))
    )
    grad_key = (key * (1.0 / math.sqrt(width))).astype(bf16).transpose(1, 0, 2)
    return grad_query, grad_key, value.astype(bf16).transpose(1, 0, 2)


def solution(mesh):
    split = P(("inner", "outer"), "head", None)
    return jax.shard_map(
        local,
        mesh=mesh,
        in_specs=(split,) * 5 + (P(), P()),
        out_specs=(split,) * 3,
        check_vma=False,
    )
```

```python
import functools
import math

import jax
import jax.numpy as jnp
from jax import lax
from jax.experimental import pallas as pl
from jax.experimental.pallas import tpu as pltpu
from jax.sharding import PartitionSpec as P

BLOCK = 128
EMPTY = -1e30
VMEM_BYTES = 20 * 1024 * 1024
ZS = 8
LIST = 128


def dot_t(a, b):
    return lax.dot_general(a, b, (((1,), (1,)), ((), ())), preferred_element_type=jnp.float32)


def lists_kernel(plans, where, span, mask, chunks):
    z, core, outer = where[0], where[1], where[2]
    for p, (near, keys, many) in enumerate(plans):
        base = p * LIST
        columns = []
        for s in keys:
            piece = z * 4 + (core ^ (s // 2)) * 2 + (outer ^ (s % 2))
            for half in range(2):
                columns.append(span[piece] * 2 + half)
        for i in range(2 * many):
            chunks[base + i] = 0
        count = jnp.int32(2 * many)
        for slot, r in enumerate(near):
            row = span[lax.rem(z + r, ZS) * 4 + core * 2 + outer] * 2
            for kb in range(len(columns)):
                halves = mask[row, columns[kb]] + 2 * mask[row + 1, columns[kb]]
                chunks[base + count] = halves * 64 + slot * 8 + kb
                count = count + jnp.minimum(halves, 1)
        for i in range(3 * many - 1):
            chunks[base + count + i] = 0
        chunks[base + LIST - 1] = (count + many - 1) // many


def lists(plans, where, span, mask):
    return pl.pallas_call(
        functools.partial(lists_kernel, plans),
        out_shape=jax.ShapeDtypeStruct((len(plans) * LIST,), jnp.int32),
        in_specs=specs(3, 0, 0),
        out_specs=pl.BlockSpec(memory_space=pltpu.SMEM),
        compiler_params=pltpu.CompilerParams(vmem_limit_bytes=2**20),
        name="lists",
    )(where, span, mask)


def unlinked(chunk, rows):
    first = lax.broadcasted_iota(jnp.int32, (1, rows), 1) < BLOCK
    halves = chunk // 64
    return (chunk // 8) % 8, chunk % 8, jnp.where(first, halves % 2, halves // 2) == 0


def gather(refs, into):
    piece = at = 0
    for ref in refs:
        into[piece, :, at : at + ref.shape[1]] = ref[...]
        at += ref.shape[1]
        if at == into.shape[2]:
            piece, at = piece + 1, 0


def zero(*refs):
    for ref in refs:
        ref[...] = jnp.zeros_like(ref)


def set_delta(x, delta, rows):
    for i in range(x.shape[0]):
        for h in range(x.shape[1]):
            parts = x[i, h, 2 * rows :, :].astype(jnp.float32)
            parts = parts[0:2] + parts[2:4] + parts[4:6]
            delta[i, h] = jnp.concatenate([parts[0:1], parts[1:2]], axis=1)


def queries_kernel(plan, n, chunks, *refs):
    p = len(refs) - 16
    x_in, kv_in = refs[:p], refs[p : p + 4]
    dq, lse = refs[p + 4], refs[p + 5]
    x, kv, kt, delta, top, total, decay, products, dprobs, dscores = refs[p + 6 :]
    heads, rows, width = kv.shape[1] // 2, kv.shape[2], kv.shape[3]
    gather(x_in, x)
    gather(kv_in, kv)
    scale = 1.0 / math.sqrt(width)
    factor = math.log2(math.e) * scale
    zero(dq, total, products, dprobs, dscores)
    top[...] = jnp.full_like(top, EMPTY)
    decay[...] = jnp.ones_like(decay)
    base = plan * LIST
    for s in range(4):
        for h in range(heads):
            for half in range(2):
                kt[s * 2 + half, h] = kv[s, h, half * BLOCK : (half + 1) * BLOCK, :].T
    set_delta(x, delta, rows)

    def body(i, _):
        at, kb, _ = unlinked(chunks[base + i], rows)
        for h in range(heads):
            dq[at, h] = dq[at, h] * decay[h] + jnp.dot(
                kt[kb, h], dscores[h], preferred_element_type=jnp.float32
            )
        at, kb, off = unlinked(chunks[base + i + 1], rows)
        for h in range(heads):
            scores = products[h] * factor
            old = top[at, h]
            new = jnp.where(off, old, jnp.maximum(old, jnp.max(scores, axis=0, keepdims=True)))
            probs = jnp.exp2(scores - jnp.where(off, -EMPTY, new))
            decay[h] = jnp.exp2(old - new)
            total[at, h] = total[at, h] * decay[h] + jnp.sum(probs, axis=0, keepdims=True)
            top[at, h] = new
            dscores[h] = (probs * (dprobs[h] - delta[at, h])).astype(jnp.bfloat16)
        at, kb, _ = unlinked(chunks[base + i + 2], rows)
        for h in range(heads):
            krows = pl.ds((kb % 2) * BLOCK, BLOCK)
            products[h] = dot_t(kv[kb // 2, h, krows, :], x[at, h, :rows])
            dprobs[h] = dot_t(kv[kb // 2, heads + h, krows, :], x[at, h, rows : 2 * rows])
        return 0

    lax.fori_loop(0, chunks[base + LIST - 1], body, 0)
    for i in range(n):
        for h in range(heads):
            some = total[i, h] > 0
            safe = jnp.where(some, total[i, h], 1.0)
            lse[i, h : h + 1] = jnp.where(some, top[i, h] + jnp.log2(safe), EMPTY)
            dq[i, h] = dq[i, h] * (scale / safe)


def keys_kernel(plan, m, extra, chunks, lse, *refs):
    n = ZS
    p = len(refs) - extra - m - 9
    x_in, kv_in = refs[:p], refs[p : p + m]
    refs = refs[p + m + extra :]
    dkv = refs[0]
    x, kv, delta, logs, products, dprobs, rounded, dscores = refs[1:]
    heads, rows, width = kv.shape[1] // 2, kv.shape[2], kv.shape[3]
    gather(x_in, x)
    gather(kv_in, kv)
    factor = math.log2(math.e) / math.sqrt(width)
    zero(dkv, products, dprobs, rounded, dscores)
    base = plan * LIST
    for i in range(n):
        for h in range(heads):
            logs[i, h] = lse[i, h : h + 1]
    set_delta(x, delta, rows)

    def body(i, _):
        for j in range(2):
            at, kb, _ = unlinked(chunks[base + i * 2 + j], rows)
            krows = pl.ds((kb % 2) * BLOCK, BLOCK)
            for h in range(heads):
                dkv[kb // 2, heads + h, krows, :] += jnp.dot(
                    rounded[j, h], x[at, h, rows : 2 * rows], preferred_element_type=jnp.float32
                )
                dkv[kb // 2, h, krows, :] += jnp.dot(
                    dscores[j, h], x[at, h, :rows], preferred_element_type=jnp.float32
                )
        for j in range(2):
            at, kb, off = unlinked(chunks[base + (i + 1) * 2 + j], rows)
            for h in range(heads):
                probs = jnp.exp2(products[j, h] * factor - jnp.where(off, -EMPTY, logs[at, h]))
                rounded[j, h] = probs.astype(jnp.bfloat16)
                dscores[j, h] = (probs * (dprobs[j, h] - delta[at, h])).astype(jnp.bfloat16)
        for j in range(2):
            at, kb, _ = unlinked(chunks[base + (i + 2) * 2 + j], rows)
            krows = pl.ds((kb % 2) * BLOCK, BLOCK)
            for h in range(heads):
                products[j, h] = dot_t(kv[kb // 2, h, krows, :], x[at, h, :rows])
                dprobs[j, h] = dot_t(kv[kb // 2, heads + h, krows, :], x[at, h, rows : 2 * rows])
        return 0

    lax.fori_loop(0, chunks[base + LIST - 1], body, 0)


def specs(smem, vmem, hbm):
    return (
        [pl.BlockSpec(memory_space=pltpu.SMEM)] * smem
        + [pl.BlockSpec(memory_space=pltpu.VMEM)] * vmem
        + [pl.BlockSpec(memory_space=pl.ANY)] * hbm
    )


def queries_part(plan, chunks, x, kv):
    heads, rows, width = kv[0].shape[0] // 2, kv[0].shape[1], kv[0].shape[2]
    tall = 2 * rows + 16
    n = len(x)
    x = [part for piece in x for part in piece]
    p = len(x)
    f32, bf16 = jnp.float32, jnp.bfloat16
    return pl.pallas_call(
        functools.partial(queries_kernel, plan, n),
        out_shape=(
            jax.ShapeDtypeStruct((n, heads, width, rows), f32),
            jax.ShapeDtypeStruct((n, heads, rows), f32),
        ),
        in_specs=specs(1, p + 4, 0),
        out_specs=(pl.BlockSpec(memory_space=pltpu.VMEM),) * 2,
        scratch_shapes=[
            pltpu.VMEM((n, heads, tall, width), bf16),
            pltpu.VMEM((4, 2 * heads, rows, width), bf16),
            pltpu.VMEM((8, heads, width, BLOCK), bf16),
            pltpu.VMEM((n, heads, 1, rows), f32),
            pltpu.VMEM((n, heads, 1, rows), f32),
            pltpu.VMEM((n, heads, 1, rows), f32),
            pltpu.VMEM((heads, 1, rows), f32),
            pltpu.VMEM((heads, BLOCK, rows), f32),
            pltpu.VMEM((heads, BLOCK, rows), f32),
            pltpu.VMEM((heads, BLOCK, rows), bf16),
        ],
        compiler_params=pltpu.CompilerParams(vmem_limit_bytes=VMEM_BYTES),
        cost_estimate=pl.CostEstimate(
            flops=n * 10**9, bytes_accessed=n * 2 * 10**6, transcendentals=n * 10**6
        ),
        name="queries_part",
    )(chunks, *x, *kv)


def keys_part(plan, chunks, lse, x, kv, after):
    heads, rows, width = kv[0].shape[0] // 2, kv[0].shape[1], kv[0].shape[2]
    tall = 2 * rows + 16
    n, m = len(x), len(kv)
    x = [part for piece in x for part in piece]
    p = len(x)
    f32, bf16 = jnp.float32, jnp.bfloat16
    return pl.pallas_call(
        functools.partial(keys_kernel, plan, m, len(after)),
        out_shape=jax.ShapeDtypeStruct((m, 2 * heads, rows, width), f32),
        in_specs=specs(1, 1 + p + m, len(after)),
        out_specs=pl.BlockSpec(memory_space=pltpu.VMEM),
        scratch_shapes=[
            pltpu.VMEM((n, heads, tall, width), bf16),
            pltpu.VMEM((m, 2 * heads, rows, width), bf16),
            pltpu.VMEM((n, heads, 1, rows), f32),
            pltpu.VMEM((n, heads, 1, rows), f32),
            pltpu.VMEM((2, heads, BLOCK, rows), f32),
            pltpu.VMEM((2, heads, BLOCK, rows), f32),
            pltpu.VMEM((2, heads, BLOCK, rows), bf16),
            pltpu.VMEM((2, heads, BLOCK, rows), bf16),
        ],
        compiler_params=pltpu.CompilerParams(vmem_limit_bytes=VMEM_BYTES),
        cost_estimate=pl.CostEstimate(
            flops=m * 2 * 10**9, bytes_accessed=m * 3 * 10**6, transcendentals=m * 10**6
        ),
        name="keys_part",
    )(chunks, lse, *x, *kv, *after)


def add_logs(a, b):
    top = jnp.maximum(a, b)
    return top + jnp.log2(jnp.exp2(a - top) + jnp.exp2(b - top))


def terms_of(x):
    terms = []
    for _ in range(3):
        term = lax.reduce_precision(x, 8, 7)
        terms.append(term.astype(jnp.bfloat16))
        x = x - term
    return terms


def local(queries, keys, values, forward_out, out_grad, span_order, block_mask):
    rows, heads, width = queries.shape
    bf16, f32 = jnp.bfloat16, jnp.float32
    inner = lax.axis_size("inner")
    zs = inner // 2
    at = lax.axis_index("inner")
    where = jnp.stack([at // 2, at % 2, lax.axis_index("outer")]).astype(jnp.int32)

    def along(x, by):
        return lax.ppermute(x, "inner", [(i, (i + 2 * by) % inner) for i in range(inner)])

    def other_core(x):
        return lax.ppermute(x, "inner", [(i, i ^ 1) for i in range(inner)])

    def other_outer(x):
        return lax.ppermute(x, "outer", [(0, 1), (1, 0)])

    delta = jnp.sum(out_grad.astype(f32) * forward_out.astype(f32), axis=2).T
    terms = jnp.stack(terms_of(delta), axis=1).reshape(heads, 3 * rows // BLOCK, BLOCK)
    terms = jnp.pad(terms, ((0, 0), (0, 16 - terms.shape[1]), (0, 0)))
    x0 = jnp.concatenate([queries.transpose(1, 0, 2), out_grad.transpose(1, 0, 2), terms], axis=1)

    keys, values, x0 = lax.optimization_barrier((keys, values, x0))
    kv0 = jnp.concatenate([keys.transpose(1, 0, 2), values.transpose(1, 0, 2)], axis=0)
    kv1 = other_outer(kv0)
    kv = [kv0, kv1, other_core(kv0), other_core(kv1)]

    half = zs // 2
    x, dq, logs = [x0] + [None] * (zs - 1), [None] * zs, [None] * zs
    for step in range(1, half):
        x[zs - step] = along(x[(zs - step + 1) % zs], 1)
        x[step] = along(x[step - 1], -1)
    far = (along(x[half + 1][:, :rows], 1), along(x[half - 1][:, rows:], -1))
    x = [(piece,) for piece in x]
    x[half] = far

    groups = [(0, 1, zs - 1)] + [(step, zs - step) for step in range(2, half)] + [(half,)]
    turns = [(1, 3), (2,), (0,)]
    plans = [(near, range(4), 1) for near in groups] + [(range(zs), pieces, 2) for pieces in turns]
    chunks = lists(plans, where, span_order, block_mask)
    for plan, near in enumerate(groups):
        part, log = queries_part(plan, chunks, [x[r] for r in near], kv)
        for i, r in enumerate(near):
            dq[r], logs[r] = part[i], log[i]

    early = jnp.pad(jnp.stack(terms_of(logs[half]), axis=1), ((0, 0), (0, 13), (0, 0)))
    early = along(jnp.concatenate([dq[half].astype(bf16), early], axis=1), -1)
    early_logs = jnp.sum(early[:, width : width + 3].astype(f32), axis=1)

    mine = jnp.stack(logs)
    lse = mine
    for d in (1, 2, 4):
        if d == 4:
            lse = lse + jnp.minimum(jnp.abs(early_logs), 0.0)
        lse = add_logs(lse, jnp.roll(along(lse, -d), d, axis=0))
    share = jnp.exp2(mine - lse)[:, :, None, :]

    down = early[:, :width].astype(f32) * jnp.exp2(early_logs - lse[half + 1])[:, None, :]
    up = None
    sums = [[]]
    for step in range(1, half):
        part = dq[half + step] * share[half + step]
        sums.append([(part + down.astype(f32)).astype(bf16)])
        down = along(sums[step][0], -1)
        part = dq[half - step] * share[half - step]
        sums[step].append((part if up is None else part + up.astype(f32)).astype(bf16))
        up = along(sums[step][1], 1)
    total = dq[0] * share[0] + down.astype(f32) + up.astype(f32)

    def keys_of(turn, after):
        return keys_part(len(groups) + turn, chunks, lse, x, [kv[s] for s in turns[turn]], after)

    away = keys_of(0, sums[1])
    away = (away[0] + other_core(away[1].astype(bf16)).astype(f32)).astype(bf16)
    theirs = keys_of(1, [away] + sums[2])[0].astype(bf16)
    away = other_outer(away)
    own = keys_of(2, [away] + sums[3])[0]
    theirs = other_core(theirs)
    last_row = jnp.minimum(jnp.abs(own[0, :1, :]), 0.0)
    grad_query = (total.transpose(2, 0, 1) + last_row).astype(bf16)
    key, value = (
        own[part] + theirs[part].astype(f32) + away[part].astype(f32)
        for part in (slice(0, heads), slice(heads, 2 * heads))
    )
    grad_key = (key * (1.0 / math.sqrt(width))).astype(bf16).transpose(1, 0, 2)
    return grad_query, grad_key, value.astype(bf16).transpose(1, 0, 2)


def solution(mesh):
    split = P(("inner", "outer"), "head", None)
    return jax.shard_map(
        local,
        mesh=mesh,
        in_specs=(split,) * 5 + (P(), P()),
        out_specs=(split,) * 3,
        check_vma=False,
    )
```
